32 devices in a mesh: groups: 2 (over y), wide: 8 (over z, x), tensor: 2 (over core).
Axes of the slice: x: 2, y: 2, z: 4, core: 2. Of those that a mesh axis runs over, the one named last changes fastest.
Arguments:
- tokens: bfloat16 [2048, 8192], P(('groups', 'wide'), 'tensor'), parts along dimension 0, may hold values from -6 to 6
- key_base_weight: bfloat16 [8192, 512], P('tensor'), may hold values from -0.0625 to 0.0625
- down_factors: bfloat16 [32, 16, 8192], P('wide', None, 'tensor'), may hold values from -0.0625 to 0.0625
- up_factors: bfloat16 [32, 16, 512], P('wide'), may hold values from -1.5 to 1.5
- segment_lengths: int32 [16, 12], P(('groups', 'wide')), parts along dimension 0, may hold values from 1 to 64, 128 in all within a row
- entry_adapters: int32 [24], P('groups'), parts along dimension 0, may hold values from 0 to 31, as said below
- adapter_store_row: int32 [32], replicated, may hold values from 0 to 31, each once
Outputs:
- projected: bfloat16 [2048, 512], P(('groups', 'wide')), parts along dimension 0
The draws below stay inside these ranges and needn't reach their ends.
There are 2 independent parts, one for each index of `groups`. The reference program is written for one: setup_inputs(seed, part) draws one part's arguments, and reference() takes and returns one part's arrays. A program takes and returns all parts, laid end to end along the dimension named above; an argument that names none is the same for every part. Nothing has to cross between parts.
Inputs may be any that keep to these rules, and one draw needn't show every extreme that they name: `entry_adapters`: 12 different adapter names. `segment_lengths`: each row holds 12 positive lengths summing to 128. `adapter_store_row`: each store row once.
All inputs are finite; a program needn't handle non-finite values.
Results may differ from the reference program's by a relative error of at most 0.001.
Values may be sent and summed in bfloat16 or wider, within the bound.
A program may use at most 64 MiB of HBM per device.

```python
import math
import jax
import jax.numpy as jnp
import numpy as np
from jax import lax

MODEL_WIDTH = 8192
KEY_OUTPUTS = 512
ADAPTER_RANK = 16
LIVE_SLOTS = 12
TOK_DEV = 128
ROWS = 1024
ADAPTER_COUNT = 32
MOST = 64
N_WIDE = 8


def draw_entry_adapters(key, part):
    key = jax.random.fold_in(key, 7)
    return jax.random.permutation(key, ADAPTER_COUNT)[:LIVE_SLOTS].astype(jnp.int32)


def block_levels(key, shape, cuts, smallest, largest):
    gain = 1.0
    for position, blocks in cuts:
        draws = jax.random.uniform(jax.random.fold_in(jax.random.fold_in(key, 6), position), (blocks,), jnp.float32, smallest / len(cuts), largest / len(cuts))
        gain = gain * jnp.repeat(jnp.exp(draws), shape[position] // blocks).reshape((-1,) + (1,) * (len(shape) - 1 - position))
    return gain


def length_profile(count, total, most, skew):
    loads = [(1 << 20) // math.isqrt(grade ** skew) + 1 for grade in range(2, count + 1)]
    surplus, holding = total - most - (count - 1), [1] * (count - 1)
    while surplus > 0:
        candidates = [i for i in range(count - 1) if holding[i] < most]
        mass, remaining = sum([loads[i] for i in candidates]), surplus
        for i in candidates:
            more = min(most - holding[i], max(1, remaining * loads[i] // mass), surplus)
            holding[i] = holding[i] + more
            surplus = surplus - more
    return np.array([most] + holding)


def uneven(rng, number_of, total, most, lean):
    if number_of == 2:
        one = jax.random.randint(rng, (), max(1, total - most), min(most, total - 1) + 1)
        return jnp.stack([one, total - one])
    sizes = jnp.asarray(length_profile(number_of, total, most, lean), jnp.int32)
    pairs = (number_of - 1) // 2
    donor, sink = sizes[1:1 + 2 * pairs:2], sizes[2:2 + 2 * pairs:2]
    margin = jnp.minimum(donor - 1, most - sink)
    passed = jax.random.randint(jax.random.fold_in(rng, 1), (pairs,), 0, 1 << 20) % (margin + 1)
    sizes = sizes.at[1:1 + 2 * pairs:2].set(donor - passed).at[2:2 + 2 * pairs:2].set(sink + passed)
    return sizes[jax.random.permutation(jax.random.fold_in(rng, 2), number_of)]


def normal_values(rng, extent, width, reach, split=(), held_as=jnp.bfloat16):
    entries = width * jax.random.normal(rng, extent, jnp.float32)
    if split:
        entries = entries * block_levels(rng, extent, split, -0.22, 0.18)
    return jnp.clip(entries, -reach, reach).astype(held_as)


def setup_inputs(seed: int = 0, part: int = 0) -> dict:
    streams_of = jax.random.split(jax.random.key(seed), 8)
    part_keys = jax.random.split(jax.random.fold_in(streams_of[7], part), 8)
    return {
        "tokens": normal_values(part_keys[0], (ROWS, MODEL_WIDTH), 1.0, 6.0, ((0, 8), (1, 2))),
        "key_base_weight": normal_values(streams_of[1], (MODEL_WIDTH, KEY_OUTPUTS), MODEL_WIDTH ** -0.5, 0.0625, ((0, 2),)),
        "down_factors": normal_values(streams_of[2], (ADAPTER_COUNT, ADAPTER_RANK, MODEL_WIDTH), MODEL_WIDTH ** -0.5, 0.0625, ((0, 8), (2, 2))),
        "up_factors": normal_values(streams_of[3], (ADAPTER_COUNT, ADAPTER_RANK, KEY_OUTPUTS), ADAPTER_RANK ** -0.5, 1.5, ((0, 8),)),
        "segment_lengths": jax.vmap(lambda own: uneven(own, LIVE_SLOTS, TOK_DEV, MOST, 2))(jax.random.split(part_keys[4], N_WIDE)).reshape((N_WIDE, LIVE_SLOTS)).astype(jnp.int32),
        "entry_adapters": draw_entry_adapters(jax.random.fold_in(jax.random.fold_in(streams_of[7], part), 71), part),
        "adapter_store_row": jax.random.permutation(streams_of[6], ADAPTER_COUNT).astype(jnp.int32),
    }


def reference(tokens, key_base_weight, down_factors, up_factors, segment_lengths, entry_adapters, adapter_store_row):
    store_positions = adapter_store_row[entry_adapters].astype(jnp.int32)
    chosen_down = down_factors[store_positions].reshape(LIVE_SLOTS * ADAPTER_RANK, MODEL_WIDTH)
    chosen_up = up_factors[store_positions].astype(jnp.float32).reshape(LIVE_SLOTS * ADAPTER_RANK, KEY_OUTPUTS)
    seg_ends = jnp.cumsum(segment_lengths, axis=1)
    row_index = jnp.arange(TOK_DEV, dtype=jnp.int32)
    entry = jnp.sum((seg_ends[:, None, :] <= row_index[None, :, None]).astype(jnp.int32), axis=2).reshape(-1)
    columns = jnp.arange(LIVE_SLOTS * ADAPTER_RANK, dtype=jnp.int32) // ADAPTER_RANK
    row_mask = (columns[None, :] == entry[:, None]).astype(jnp.float32)
    shrink = jnp.dot(tokens, chosen_down.T, preferred_element_type=jnp.float32) * row_mask
    base = jnp.dot(tokens, key_base_weight, preferred_element_type=jnp.float32)
    adapted = jnp.dot(shrink, chosen_up, precision=lax.Precision.HIGHEST)
    return (base + adapted).astype(jnp.bfloat16)
```

```python
import functools

import jax
import jax.numpy as jnp
from jax import lax
from jax.experimental import pallas as pl
from jax.experimental.pallas import tpu as pltpu
from jax.sharding import PartitionSpec as P

MESH = pl.DeviceIdType.MESH
F32 = jnp.float32
BF16 = jnp.bfloat16
GATHER_LIMIT = 8 << 20
W_PIECES = 4


def kernel(
    n,
    tok_hbm,
    w_hbm,
    down_hbm,
    up_hbm,
    seg_ref,
    names_ref,
    rows_ref,
    out_ref,
    tok,
    weight,
    base,
    base_in,
    level_tok,
    level_home,
    chunks,
    ups,
    ups_other,
    part,
    part_in,
    half,
    local_sem,
    w_sem,
    home_send,
    home_recv,
    tok_send,
    tok_recv,
    up_send,
    up_recv,
    down_send,
    down_recv,
    upy_sem,
    base_sem,
    part_send,
    part_recv,
    half_sem,
):
    y = lax.axis_index("groups")
    w = lax.axis_index("wide")
    t = lax.axis_index("tensor")
    x = lax.rem(w, 2)
    rows, width = tok_hbm.shape
    held, rank, _ = down_hbm.shape
    outputs = w_hbm.shape[1]
    quarter = width // 4
    narrow = outputs // 4
    entries = names_ref.shape[0]

    def level_peer(m):
        px = 1 - x if m & 1 else x
        py = 1 - y if m & 2 else y
        return py, w - x + px, px

    def quarter_of(py, px):
        return pl.ds(pl.multiple_of((py * 2 + px) * quarter, quarter), quarter)

    def columns(core, yy):
        return pl.ds(pl.multiple_of((core * 2 + yy) * narrow, narrow), narrow)

    mine = quarter_of(y, x)
    local = [
        pltpu.make_async_copy(tok_hbm, tok, local_sem.at[0]),
        pltpu.make_async_copy(tok_hbm.at[:, mine], level_tok.at[pl.ds(0, rows)], local_sem.at[1]),
        pltpu.make_async_copy(down_hbm.at[:, :, mine], chunks.at[0], local_sem.at[2]),
        pltpu.make_async_copy(up_hbm.at[:, :, columns(t, y)], ups.at[0], local_sem.at[3]),
    ]
    piece = width // W_PIECES
    w_copies = [
        pltpu.make_async_copy(
            w_hbm.at[pl.ds(i * piece, piece)], weight.at[pl.ds(i * piece, piece)], w_sem.at[i]
        )
        for i in range(W_PIECES)
    ]

    barrier = pltpu.get_barrier_semaphore()
    peers = [(y, lax.rem(w + k, n), t) for k in range(1, n)]
    peers += [(level_peer(m)[0], level_peer(m)[1], t) for m in (2, 3)]
    peers += [(level_peer(m)[0], level_peer(m)[1], 1 - t) for m in range(4)]
    for peer in peers:
        pl.semaphore_signal(barrier, inc=1, device_id=peer, device_id_type=MESH)
    for copy in local + w_copies:
        copy.start()

    lane = lax.broadcasted_iota(jnp.int32, (8, rows), 1)
    end = seg_ref[0, 0]
    home = jnp.full((8, rows), rows_ref[names_ref[0]].astype(F32), F32)
    for e in range(1, entries):
        home = jnp.where(lane >= end, rows_ref[names_ref[e]].astype(F32), home)
        end = end + seg_ref[0, e]
    level_home[0] = home
    pl.semaphore_wait(barrier, len(peers))

    def remote(src, dst, send, recv, peer):
        return pltpu.make_async_remote_copy(
            src_ref=src, dst_ref=dst, send_sem=send, recv_sem=recv, device_id=peer, device_id_type=MESH
        )

    home_copies, tok_copies = [], []
    for m in range(1, 4):
        py, pw, px = level_peer(m)
        home_copies.append(
            remote(level_home.at[0], level_home.at[m], home_send.at[m], home_recv.at[m], (py, pw, t))
        )
        tok_copies.append(
            remote(
                tok_hbm.at[:, quarter_of(py, px)],
                level_tok.at[pl.ds(m * rows, rows)],
                tok_send.at[m],
                tok_recv.at[m],
                (py, pw, t),
            )
        )
    up_copies, down_copies = [], []
    for k in range(1, n):
        pw = lax.rem(w + k, n)
        up_copies.append(
            remote(up_hbm.at[:, :, columns(t, y)], ups.at[k], up_send.at[k], up_recv.at[k], (y, pw, t))
        )
        down_copies.append(
            remote(
                down_hbm.at[:, :, quarter_of(y, lax.rem(pw, 2))],
                chunks.at[k],
                down_send.at[k],
                down_recv.at[k],
                (y, pw, t),
            )
        )
    order = sorted(range(1, n), key=lambda k: -min(k, n - k))
    for copy in home_copies:
        copy.start()
    for k in order:
        down_copies[k - 1].start()
    for copy in tok_copies:
        copy.start()
    for copy in up_copies:
        copy.start()

    local[0].wait()
    for i in range(W_PIECES):
        w_copies[i].wait()
        term = jnp.dot(
            tok[:, i * piece : (i + 1) * piece],
            weight[i * piece : (i + 1) * piece, :],
            preferred_element_type=F32,
        )
        for c in range(4):
            cut = term[:, c * narrow : (c + 1) * narrow]
            base[c] = cut if i == 0 else base[c] + cut
    base_copy = remote(
        base.at[pl.ds((1 - t) * 2, 2)], base_in, base_sem.at[0], base_sem.at[1], (y, w, 1 - t)
    )
    base_copy.start()

    for copy in home_copies:
        copy.wait_recv()
    for copy in tok_copies:
        copy.wait_recv()
    for copy in local[1:]:
        copy.wait()
    level_rows = 4 * rows
    home_all = jnp.concatenate([level_home[m, 0:1, :] for m in range(4)], axis=1)
    home_all = jnp.broadcast_to(home_all, (rank, level_rows))
    total = jnp.zeros((rank, level_rows), F32)
    for k in [0] + order[::-1]:
        if k:
            down_copies[k - 1].wait_recv()
        product = lax.dot_general(
            chunks[k].reshape(held * rank, quarter),
            level_tok[...],
            (((1,), (1,)), ((), ())),
            preferred_element_type=F32,
        )
        first = lax.rem(w + n - k, n) * held
        for i in range(held):
            row = (first + i).astype(F32)
            total = total + jnp.where(home_all == row, product[i * rank : (i + 1) * rank], 0.0)
    for m in range(4):
        part[m] = total[:, m * rows : (m + 1) * rows]
    part_copies = []
    for m in range(4):
        py, pw, _ = level_peer(m)
        for other in range(2):
            if m == 0 and other == 0:
                continue
            slot = 2 * m + other
            core = 1 - t if other else t
            part_copies.append(
                remote(part.at[m], part_in.at[slot], part_send.at[slot], part_recv.at[slot], (py, pw, core))
            )
    for copy in part_copies:
        copy.start()

    for copy in up_copies:
        copy.wait_recv()
    up_copy = remote(ups, ups_other, upy_sem.at[0], upy_sem.at[1], (1 - y, w, t))
    up_copy.start()

    shrink = part[0]
    for slot, copy in enumerate(part_copies, 1):
        copy.wait_recv()
        shrink = shrink + part_in[slot]
    own_home = jnp.broadcast_to(level_home[0, 0:1, :], (rank, rows))
    spread = []
    for k in range(n):
        first = lax.rem(w + n - k, n) * held
        for i in range(held):
            spread.append(jnp.where(own_home == (first + i).astype(F32), shrink, 0.0))
    spread = jnp.transpose(jnp.concatenate(spread, axis=0))
    high = spread.astype(BF16)
    low = (spread - high.astype(F32)).astype(BF16)

    def expand(factors):
        flat = factors.reshape(n * held * rank, narrow)
        return jnp.dot(high, flat, preferred_element_type=F32) + jnp.dot(
            low, flat, preferred_element_type=F32
        )

    base_copy.wait_recv()
    own = expand(ups[...]) + base[t * 2 + y] + base_in[y]
    half[t, y] = own.astype(BF16)
    up_copy.wait_recv()
    other = expand(ups_other[...]) + base[t * 2 + 1 - y] + base_in[1 - y]
    half[t, 1 - y] = other.astype(BF16)
    half_copy = remote(half.at[t], half.at[t], half_sem.at[0], half_sem.at[1], (y, w, 1 - t))
    half_copy.start()
    for copy in home_copies + tok_copies + up_copies + down_copies + part_copies:
        copy.wait_send()
    base_copy.wait_send()
    up_copy.wait_send()
    half_copy.wait()
    for c in range(4):
        out_ref[:, c * narrow : (c + 1) * narrow] = half[c // 2, c % 2]


def by_gather(n, tokens, key_base_weight, down_factors, up_factors, segment_lengths, entry_adapters, adapter_store_row):
    rows, width = tokens.shape
    held, rank, _ = down_factors.shape
    outputs = key_base_weight.shape[1]
    quarter, narrow = width // 4, outputs // 4
    anywhere = pl.BlockSpec(memory_space=pl.ANY)
    scalars = pl.BlockSpec(memory_space=pltpu.SMEM)
    dma = pltpu.SemaphoreType.DMA
    return pl.pallas_call(
        functools.partial(kernel, n),
        out_shape=jax.ShapeDtypeStruct((rows, outputs), BF16),
        in_specs=[anywhere] * 4 + [scalars] * 3,
        out_specs=pl.BlockSpec(memory_space=pltpu.VMEM),
        scratch_shapes=[
            pltpu.VMEM((rows, width), BF16),
            pltpu.VMEM((width, outputs), BF16),
            pltpu.VMEM((4, rows, narrow), F32),
            pltpu.VMEM((2, rows, narrow), F32),
            pltpu.VMEM((4 * rows, quarter), BF16),
            pltpu.VMEM((4, 8, rows), F32),
            pltpu.VMEM((n, held, rank, quarter), BF16),
            pltpu.VMEM((n, held, rank, narrow), BF16),
            pltpu.VMEM((n, held, rank, narrow), BF16),
            pltpu.VMEM((4, rank, rows), F32),
            pltpu.VMEM((8, rank, rows), F32),
            pltpu.VMEM((2, 2, rows, narrow), BF16),
            dma((4,)),
            dma((W_PIECES,)),
            dma((4,)),
            dma((4,)),
            dma((4,)),
            dma((4,)),
            dma((n,)),
            dma((n,)),
            dma((n,)),
            dma((n,)),
            dma((2,)),
            dma((2,)),
            dma((8,)),
            dma((8,)),
            dma((2,)),
        ],
        compiler_params=pltpu.CompilerParams(
            collective_id=0, has_side_effects=True, vmem_limit_bytes=40 << 20
        ),
    )(tokens, key_base_weight, down_factors, up_factors, segment_lengths, entry_adapters, adapter_store_row)


def by_sum(tokens, key_base_weight, down_factors, up_factors, segment_lengths, entry_adapters, adapter_store_row):
    held, rank, width = down_factors.shape
    outputs = up_factors.shape[2]
    entries = entry_adapters.shape[0]
    rows = tokens.shape[0]
    positions = adapter_store_row[entry_adapters]
    mine = (positions // held == lax.axis_index("wide"))[:, None, None]
    places = positions % held
    down = jnp.where(mine, down_factors[places], jnp.zeros((), BF16))
    up = jnp.where(mine, up_factors[places], jnp.zeros((), BF16))
    down, up = lax.psum((down, up), "wide")
    ends = jnp.cumsum(segment_lengths[0])
    index = jnp.arange(rows, dtype=jnp.int32)
    entry = jnp.sum((ends[None, :] <= index[:, None]).astype(jnp.int32), axis=1)
    column = jnp.arange(entries * rank, dtype=jnp.int32) // rank
    mask = (column[None, :] == entry[:, None]).astype(F32)
    shrink = mask * lax.dot_general(
        tokens,
        down.reshape(entries * rank, width),
        (((1,), (1,)), ((), ())),
        preferred_element_type=F32,
    )
    base = jnp.dot(tokens, key_base_weight, preferred_element_type=F32)
    base, shrink = lax.psum((base, shrink), "tensor")
    flat = up.reshape(entries * rank, outputs).astype(F32)
    return (base + jnp.dot(shrink, flat, precision=lax.Precision.HIGHEST)).astype(BF16)


def solution(mesh):
    n = mesh.shape["wide"]

    def per_device(tokens, key_base_weight, down_factors, *rest):
        gathered = n * down_factors.size * 2 // 4
        paired = mesh.shape["groups"] == 2 and mesh.shape["tensor"] == 2 and n % 2 == 0
        if paired and gathered <= GATHER_LIMIT:
            return by_gather(n, tokens, key_base_weight, down_factors, *rest)
        return by_sum(tokens, key_base_weight, down_factors, *rest)

    in_specs = (
        P(("groups", "wide"), "tensor"),
        P("tensor", None),
        P("wide", None, "tensor"),
        P("wide", None, None),
        P(("groups", "wide"), None),
        P("groups"),
        P(),
    )
    out_specs = P(("groups", "wide"), None)
    return jax.shard_map(
        per_device, mesh=mesh, in_specs=in_specs, out_specs=out_specs, check_vma=False
    )
```

```python
import functools

import jax
import jax.numpy as jnp
from jax import lax
from jax.experimental import pallas as pl
from jax.experimental.pallas import tpu as pltpu
from jax.sharding import PartitionSpec as P

MESH = pl.DeviceIdType.MESH
F32 = jnp.float32
BF16 = jnp.bfloat16
GATHER_LIMIT = 8 << 20
W_PIECES = 4


def kernel(
    n,
    tok_hbm,
    w_hbm,
    down_hbm,
    up_hbm,
    seg_ref,
    names_ref,
    rows_ref,
    out_ref,
    tok,
    weight,
    base,
    base_in,
    level_tok,
    level_home,
    chunks,
    ups,
    ups_other,
    part,
    part_in,
    half,
    local_sem,
    w_sem,
    home_send,
    home_recv,
    tok_send,
    tok_recv,
    up_send,
    up_recv,
    down_send,
    down_recv,
    upy_sem,
    base_sem,
    part_send,
    part_recv,
    half_sem,
):
    y = lax.axis_index("groups")
    w = lax.axis_index("wide")
    t = lax.axis_index("tensor")
    x = lax.rem(w, 2)
    rows, width = tok_hbm.shape
    held, rank, _ = down_hbm.shape
    outputs = w_hbm.shape[1]
    quarter = width // 4
    narrow = outputs // 4
    entries = names_ref.shape[0]

    def level_peer(m):
        px = 1 - x if m & 1 else x
        py = 1 - y if m & 2 else y
        return py, w - x + px, px

    def quarter_of(py, px):
        return pl.ds(pl.multiple_of((py * 2 + px) * quarter, quarter), quarter)

    def columns(core, yy):
        return pl.ds(pl.multiple_of((core * 2 + yy) * narrow, narrow), narrow)

    mine = quarter_of(y, x)
    local = [
        pltpu.make_async_copy(tok_hbm, tok, local_sem.at[0]),
        pltpu.make_async_copy(tok_hbm.at[:, mine], level_tok.at[pl.ds(0, rows)], local_sem.at[1]),
        pltpu.make_async_copy(down_hbm.at[:, :, mine], chunks.at[0], local_sem.at[2]),
        pltpu.make_async_copy(up_hbm.at[:, :, columns(t, y)], ups.at[0], local_sem.at[3]),
    ]
    piece = width // W_PIECES
    w_copies = [
        pltpu.make_async_copy(
            w_hbm.at[pl.ds(i * piece, piece)], weight.at[pl.ds(i * piece, piece)], w_sem.at[i]
        )
        for i in range(W_PIECES)
    ]

    barrier = pltpu.get_barrier_semaphore()
    peers = [(y, lax.rem(w + k, n), t) for k in range(1, n)]
    peers += [(level_peer(m)[0], level_peer(m)[1], t) for m in (2, 3)]
    peers += [(level_peer(m)[0], level_peer(m)[1], 1 - t) for m in range(4)]
    for peer in peers:
        pl.semaphore_signal(barrier, inc=1, device_id=peer, device_id_type=MESH)
    for copy in local + w_copies:
        copy.start()

    lane = lax.broadcasted_iota(jnp.int32, (8, rows), 1)
    end = seg_ref[0, 0]
    home = jnp.full((8, rows), rows_ref[names_ref[0]].astype(F32), F32)
    for e in range(1, entries):
        home = jnp.where(lane >= end, rows_ref[names_ref[e]].astype(F32), home)
        end = end + seg_ref[0, e]
    level_home[0] = home
    pl.semaphore_wait(barrier, len(peers))

    def remote(src, dst, send, recv, peer):
        return pltpu.make_async_remote_copy(
            src_ref=src, dst_ref=dst, send_sem=send, recv_sem=recv, device_id=peer, device_id_type=MESH
        )

    home_copies, tok_copies = [], []
    for m in range(1, 4):
        py, pw, px = level_peer(m)
        home_copies.append(
            remote(level_home.at[0], level_home.at[m], home_send.at[m], home_recv.at[m], (py, pw, t))
        )
        tok_copies.append(
            remote(
                tok_hbm.at[:, quarter_of(py, px)],
                level_tok.at[pl.ds(m * rows, rows)],
                tok_send.at[m],
                tok_recv.at[m],
                (py, pw, t),
            )
        )
    up_copies, down_copies = [], []
    for k in range(1, n):
        pw = lax.rem(w + k, n)
        up_copies.append(
            remote(up_hbm.at[:, :, columns(t, y)], ups.at[k], up_send.at[k], up_recv.at[k], (y, pw, t))
        )
        down_copies.append(
            remote(
                down_hbm.at[:, :, quarter_of(y, lax.rem(pw, 2))],
                chunks.at[k],
                down_send.at[k],
                down_recv.at[k],
                (y, pw, t),
            )
        )
    order = sorted(range(1, n), key=lambda k: -min(k, n - k))
    for copy in home_copies:
        copy.start()
    for k in order:
        down_copies[k - 1].start()
    for copy in tok_copies:
        copy.start()
    for copy in up_copies:
        copy.start()

    local[0].wait()
    for i in range(W_PIECES):
        w_copies[i].wait()
        term = jnp.dot(
            tok[:, i * piece : (i + 1) * piece],
            weight[i * piece : (i + 1) * piece, :],
            preferred_element_type=F32,
        )
        for c in range(4):
            cut = term[:, c * narrow : (c + 1) * narrow]
            base[c] = cut if i == 0 else base[c] + cut
    base_copy = remote(
        base.at[pl.ds((1 - t) * 2, 2)], base_in, base_sem.at[0], base_sem.at[1], (y, w, 1 - t)
    )
    base_copy.start()

    for copy in home_copies:
        copy.wait_recv()
    for copy in tok_copies:
        copy.wait_recv()
    for copy in local[1:]:
        copy.wait()
    level_rows = 4 * rows
    home_all = jnp.concatenate([level_home[m, 0:1, :] for m in range(4)], axis=1)
    home_all = jnp.broadcast_to(home_all, (rank, level_rows))
    total = jnp.zeros((rank, level_rows), F32)
    for k in [0] + order[::-1]:
        if k:
            down_copies[k - 1].wait_recv()
        product = lax.dot_general(
            chunks[k].reshape(held * rank, quarter),
            level_tok[...],
            (((1,), (1,)), ((), ())),
            preferred_element_type=F32,
        )
        first = lax.rem(w + n - k, n) * held
        for i in range(held):
            row = (first + i).astype(F32)
            total = total + jnp.where(home_all == row, product[i * rank : (i + 1) * rank], 0.0)
    for m in range(4):
        part[m] = total[:, m * rows : (m + 1) * rows]
    part_copies = []
    for m in range(4):
        py, pw, _ = level_peer(m)
        for other in range(2):
            if m == 0 and other == 0:
                continue
            slot = 2 * m + other
            core = 1 - t if other else t
            part_copies.append(
                remote(part.at[m], part_in.at[slot], part_send.at[slot], part_recv.at[slot], (py, pw, core))
            )
    for copy in part_copies:
        copy.start()

    for copy in up_copies:
        copy.wait_recv()
    up_copy = remote(ups, ups_other, upy_sem.at[0], upy_sem.at[1], (1 - y, w, t))
    up_copy.start()

    shrink = part[0]
    for slot, copy in enumerate(part_copies, 1):
        copy.wait_recv()
        shrink = shrink + part_in[slot]
    own_home = jnp.broadcast_to(level_home[0, 0:1, :], (rank, rows))
    spread = []
    for k in range(n):
        first = lax.rem(w + n - k, n) * held
        for i in range(held):
            spread.append(jnp.where(own_home == (first + i).astype(F32), shrink, 0.0))
    spread = jnp.transpose(jnp.concatenate(spread, axis=0))
    high = spread.astype(BF16)
    low = (spread - high.astype(F32)).astype(BF16)

    def expand(factors):
        flat = factors.reshape(n * held * rank, narrow)
        return jnp.dot(high, flat, preferred_element_type=F32) + jnp.dot(
            low, flat, preferred_element_type=F32
        )

    base_copy.wait_recv()
    own = expand(ups[...]) + base[t * 2 + y] + base_in[y]
    half[t, y] = own.astype(BF16)
    up_copy.wait_recv()
    other = expand(ups_other[...]) + base[t * 2 + 1 - y] + base_in[1 - y]
    half[t, 1 - y] = other.astype(BF16)
    half_copy = remote(half.at[t], half.at[t], half_sem.at[0], half_sem.at[1], (y, w, 1 - t))
    half_copy.start()
    for copy in home_copies + tok_copies + up_copies + down_copies + part_copies:
        copy.wait_send()
    base_copy.wait_send()
    up_copy.wait_send()
    half_copy.wait()
    for c in range(4):
        out_ref[:, c * narrow : (c + 1) * narrow] = half[c // 2, c % 2]


def by_gather(n, tokens, key_base_weight, down_factors, up_factors, segment_lengths, entry_adapters, adapter_store_row):
    rows, width = tokens.shape
    held, rank, _ = down_factors.shape
    outputs = key_base_weight.shape[1]
    quarter, narrow = width // 4, outputs // 4
    anywhere = pl.BlockSpec(memory_space=pl.ANY)
    scalars = pl.BlockSpec(memory_space=pltpu.SMEM)
    dma = pltpu.SemaphoreType.DMA
    return pl.pallas_call(
        functools.partial(kernel, n),
        out_shape=jax.ShapeDtypeStruct((rows, outputs), BF16),
        in_specs=[anywhere] * 4 + [scalars] * 3,
        out_specs=pl.BlockSpec(memory_space=pltpu.VMEM),
        scratch_shapes=[
            pltpu.VMEM((rows, width), BF16),
            pltpu.VMEM((width, outputs), BF16),
            pltpu.VMEM((4, rows, narrow), F32),
            pltpu.VMEM((2, rows, narrow), F32),
            pltpu.VMEM((4 * rows, quarter), BF16),
            pltpu.VMEM((4, 8, rows), F32),
            pltpu.VMEM((n, held, rank, quarter), BF16),
            pltpu.VMEM((n, held, rank, narrow), BF16),
            pltpu.VMEM((n, held, rank, narrow), BF16),
            pltpu.VMEM((4, rank, rows), F32),
            pltpu.VMEM((8, rank, rows), F32),
            pltpu.VMEM((2, 2, rows, narrow), BF16),
            dma((4,)),
            dma((W_PIECES,)),
            dma((4,)),
            dma((4,)),
            dma((4,)),
            dma((4,)),
            dma((n,)),
            dma((n,)),
            dma((n,)),
            dma((n,)),
            dma((2,)),
            dma((2,)),
            dma((8,)),
            dma((8,)),
            dma((2,)),
        ],
        compiler_params=pltpu.CompilerParams(
            collective_id=0, has_side_effects=True, vmem_limit_bytes=60 << 20
        ),
    )(tokens, key_base_weight, down_factors, up_factors, segment_lengths, entry_adapters, adapter_store_row)


def by_sum(tokens, key_base_weight, down_factors, up_factors, segment_lengths, entry_adapters, adapter_store_row):
    held, rank, width = down_factors.shape
    outputs = up_factors.shape[2]
    entries = entry_adapters.shape[0]
    rows = tokens.shape[0]
    positions = adapter_store_row[entry_adapters]
    mine = (positions // held == lax.axis_index("wide"))[:, None, None]
    places = positions % held
    down = jnp.where(mine, down_factors[places], jnp.zeros((), BF16))
    up = jnp.where(mine, up_factors[places], jnp.zeros((), BF16))
    down, up = lax.psum((down, up), "wide")
    ends = jnp.cumsum(segment_lengths[0])
    index = jnp.arange(rows, dtype=jnp.int32)
    entry = jnp.sum((ends[None, :] <= index[:, None]).astype(jnp.int32), axis=1)
    column = jnp.arange(entries * rank, dtype=jnp.int32) // rank
    mask = (column[None, :] == entry[:, None]).astype(F32)
    shrink = mask * lax.dot_general(
        tokens,
        down.reshape(entries * rank, width),
        (((1,), (1,)), ((), ())),
        preferred_element_type=F32,
    )
    base = jnp.dot(tokens, key_base_weight, preferred_element_type=F32)
    base, shrink = lax.psum((base, shrink), "tensor")
    flat = up.reshape(entries * rank, outputs).astype(F32)
    return (base + jnp.dot(shrink, flat, precision=lax.Precision.HIGHEST)).astype(BF16)


def solution(mesh):
    n = mesh.shape["wide"]

    def per_device(tokens, key_base_weight, down_factors, *rest):
        gathered = n * down_factors.size * 2 // 4
        paired = mesh.shape["groups"] == 2 and mesh.shape["tensor"] == 2 and n % 2 == 0
        if paired and gathered <= GATHER_LIMIT:
            return by_gather(n, tokens, key_base_weight, down_factors, *rest)
        return by_sum(tokens, key_base_weight, down_factors, *rest)

    in_specs = (
        P(("groups", "wide"), "tensor"),
        P("tensor", None),
        P("wide", None, "tensor"),
        P("wide", None, None),
        P(("groups", "wide"), None),
        P("groups"),
        P(),
    )
    out_specs = P(("groups", "wide"), None)
    return jax.shard_map(
        per_device, mesh=mesh, in_specs=in_specs, out_specs=out_specs, check_vma=False
    )
```

```python
import functools

import jax
import jax.numpy as jnp
from jax import lax
from jax.experimental import pallas as pl
from jax.experimental.pallas import tpu as pltpu
from jax.sharding import PartitionSpec as P

MESH = pl.DeviceIdType.MESH
F32 = jnp.float32
BF16 = jnp.bfloat16
GATHER_LIMIT = 8 << 20
W_PIECES = 4


def kernel(
    n,
    tok_hbm,
    w_hbm,
    down_hbm,
    up_hbm,
    seg_ref,
    names_ref,
    rows_ref,
    out_ref,
    tok,
    weight,
    base,
    base_in,
    level_tok,
    level_home,
    chunks,
    ups,
    total,
    part,
    part_in,
    half,
    local_sem,
    w_sem,
    home_send,
    home_recv,
    tok_send,
    tok_recv,
    up_send,
    up_recv,
    down_send,
    down_recv,
    x_sem,
    relay_send,
    upl_send,
    upl_recv,
    base_sem,
    part_send,
    part_recv,
    half_sem,
):
    y = lax.axis_index("groups")
    w = lax.axis_index("wide")
    t = lax.axis_index("tensor")
    x = lax.rem(w, 2)
    z = w // 2
    levels = n // 2
    rows, width = tok_hbm.shape
    held, rank, _ = down_hbm.shape
    outputs = w_hbm.shape[1]
    quarter = width // 4
    narrow = outputs // 4
    entries = names_ref.shape[0]

    def level_peer(m):
        px = 1 - x if m & 1 else x
        py = 1 - y if m & 2 else y
        return py, w - x + px, px

    def quarter_of(py, px):
        return pl.ds(pl.multiple_of((py * 2 + px) * quarter, quarter), quarter)

    def columns(core, yy):
        return pl.ds(pl.multiple_of((core * 2 + yy) * narrow, narrow), narrow)

    mine = quarter_of(y, x)
    local = [
        pltpu.make_async_copy(tok_hbm, tok, local_sem.at[0]),
        pltpu.make_async_copy(tok_hbm.at[:, mine], level_tok.at[pl.ds(0, rows)], local_sem.at[1]),
        pltpu.make_async_copy(down_hbm.at[:, :, mine], chunks.at[z, 0], local_sem.at[2]),
        pltpu.make_async_copy(up_hbm.at[:, :, columns(t, y)], ups.at[0, 0], local_sem.at[3]),
    ]
    piece = width // W_PIECES
    w_copies = [
        pltpu.make_async_copy(
            w_hbm.at[pl.ds(i * piece, piece)], weight.at[pl.ds(i * piece, piece)], w_sem.at[i]
        )
        for i in range(W_PIECES)
    ]

    barrier = pltpu.get_barrier_semaphore()
    peers = [(y, lax.rem(z + k, levels) * 2 + x, t) for k in range(1, levels)]
    peers += [(level_peer(m)[0], level_peer(m)[1], t) for m in range(1, 4)]
    peers += [(level_peer(m)[0], level_peer(m)[1], 1 - t) for m in range(4)]
    for peer in peers:
        pl.semaphore_signal(barrier, inc=1, device_id=peer, device_id_type=MESH)
    for copy in local + w_copies:
        copy.start()

    lane = lax.broadcasted_iota(jnp.int32, (8, rows), 1)
    end = seg_ref[0, 0]
    home = jnp.full((8, rows), rows_ref[names_ref[0]].astype(F32), F32)
    for e in range(1, entries):
        home = jnp.where(lane >= end, rows_ref[names_ref[e]].astype(F32), home)
        end = end + seg_ref[0, e]
    level_home[0] = home

    local[0].wait()
    for i in range(W_PIECES):
        w_copies[i].wait()
        term = jnp.dot(
            tok[:, i * piece : (i + 1) * piece],
            weight[i * piece : (i + 1) * piece, :],
            preferred_element_type=F32,
        )
        for c in range(4):
            cut = term[:, c * narrow : (c + 1) * narrow]
            base[c] = cut if i == 0 else base[c] + cut
    pl.semaphore_wait(barrier, len(peers))

    def remote(src, dst, send, recv, peer):
        return pltpu.make_async_remote_copy(
            src_ref=src, dst_ref=dst, send_sem=send, recv_sem=recv, device_id=peer, device_id_type=MESH
        )

    home_copies, tok_copies = [], []
    for m in range(1, 4):
        py, pw, px = level_peer(m)
        home_copies.append(
            remote(level_home.at[0], level_home.at[m], home_send.at[m], home_recv.at[m], (py, pw, t))
        )
        tok_copies.append(
            remote(
                tok_hbm.at[:, quarter_of(py, px)],
                level_tok.at[pl.ds(m * rows, rows)],
                tok_send.at[m],
                tok_recv.at[m],
                (py, pw, t),
            )
        )
    up_copies = []
    for k in range(1, levels):
        up_copies.append(
            remote(
                up_hbm.at[:, :, columns(t, y)],
                ups.at[0, k],
                up_send.at[k],
                up_recv.at[k],
                (y, lax.rem(z + k, levels) * 2 + x, t),
            )
        )
    x_copy = remote(
        down_hbm.at[:, :, quarter_of(y, 1 - x)],
        chunks.at[z, 1],
        x_sem,
        down_recv.at[z, 1],
        (y, w - x + 1 - x, t),
    )

    def down_copy(part_of, delta):
        source = chunks.at[z, 1] if part_of else down_hbm.at[:, :, mine]
        return remote(
            source,
            chunks.at[z, part_of],
            down_send.at[delta + 2, part_of],
            down_recv.at[z, part_of],
            (y, w + 2 * delta, t),
        )

    def relay_copy(part_of, distance, sign):
        source = z + sign * distance
        return remote(
            chunks.at[source, part_of],
            chunks.at[source, part_of],
            relay_send.at[distance, (sign + 1) // 2, part_of],
            down_recv.at[source, part_of],
            (y, w - 2 * sign, t),
        )

    def arrival(level, part_of):
        return pltpu.make_async_copy(
            chunks.at[level, part_of], chunks.at[level, part_of], down_recv.at[level, part_of]
        )

    deltas = [d for d in (2, -2, 1, -1) if abs(d) < levels]
    relays = [(d, sign) for d in range(2, levels - 1) for sign in (1, -1)]

    def level_exists(delta):
        return jnp.logical_and(z + delta >= 0, z + delta < levels)

    def relaying(distance, sign):
        return jnp.logical_and(level_exists(sign * distance), level_exists(-sign))

    for copy in home_copies:
        copy.start()
    x_copy.start()
    for copy in up_copies:
        copy.start()
    for delta in deltas:

        @pl.when(level_exists(delta))
        def _():
            down_copy(0, delta).start()

    for copy in tok_copies:
        copy.start()
    base_copy = remote(
        base.at[pl.ds((1 - t) * 2, 2)], base_in, base_sem.at[0], base_sem.at[1], (y, w, 1 - t)
    )
    base_copy.start()
    x_copy.wait_recv()
    for delta in deltas:

        @pl.when(level_exists(delta))
        def _():
            down_copy(1, delta).start()

    for distance, sign in relays:

        @pl.when(relaying(distance, sign))
        def _():
            for part_of in range(2):
                copy = relay_copy(part_of, distance, sign)
                arrival(z + sign * distance, part_of).wait()
                copy.start()

    for copy in up_copies:
        copy.wait_recv()
    local[3].wait()
    level_ups = []
    for m in range(1, 4):
        py, pw, _ = level_peer(m)
        level_ups.append(remote(ups.at[0], ups.at[m], upl_send.at[m], upl_recv.at[m], (py, pw, t)))
    for copy in level_ups:
        copy.start()

    for copy in home_copies:
        copy.wait_recv()
    for copy in tok_copies:
        copy.wait_recv()
    for copy in local[1:3]:
        copy.wait()
    level_rows = 4 * rows
    home_all = jnp.concatenate([level_home[m, 0:1, :] for m in range(4)], axis=1)
    home_all = jnp.broadcast_to(home_all, (rank, level_rows))
    total[...] = jnp.zeros((rank, level_rows), F32)

    def add_shrink(level, part_of):
        product = lax.dot_general(
            chunks[level, part_of].reshape(held * rank, quarter),
            level_tok[...],
            (((1,), (1,)), ((), ())),
            preferred_element_type=F32,
        )
        first = (level * 2 + (1 - x if part_of else x)) * held
        kept = total[...]
        for i in range(held):
            row = (first + i).astype(F32)
            kept = kept + jnp.where(home_all == row, product[i * rank : (i + 1) * rank], 0.0)
        total[...] = kept

    for part_of in range(2):
        add_shrink(z, part_of)
    low_end = z < levels // 2
    ahead = jnp.where(low_end, z, levels - 1 - z)
    for j in range(levels - 1):
        place = j + (j >= ahead).astype(jnp.int32)
        level = jnp.where(low_end, place, levels - 1 - place)
        for part_of in range(2):
            forwarded = jnp.bool_(False)
            for distance, sign in relays:
                here = jnp.logical_and(relaying(distance, sign), level == z + sign * distance)
                forwarded = jnp.logical_or(forwarded, here)

            @pl.when(jnp.logical_not(forwarded))
            def _():
                arrival(level, part_of).wait()

            add_shrink(level, part_of)
    for m in range(4):
        part[m] = total[:, m * rows : (m + 1) * rows]
    part_copies = []
    for m in range(4):
        py, pw, _ = level_peer(m)
        for other in range(2):
            if m == 0 and other == 0:
                continue
            slot = 2 * m + other
            core = 1 - t if other else t
            part_copies.append(
                remote(part.at[m], part_in.at[slot], part_send.at[slot], part_recv.at[slot], (py, pw, core))
            )
    for copy in part_copies:
        copy.start()

    shrink = part[0]
    for slot, copy in enumerate(part_copies, 1):
        copy.wait_recv()
        shrink = shrink + part_in[slot]
    own_home = jnp.broadcast_to(level_home[0, 0:1, :], (rank, rows))
    spread = []
    for px in (x, 1 - x):
        for k in range(levels):
            first = (lax.rem(z + levels - k, levels) * 2 + px) * held
            for i in range(held):
                spread.append(jnp.where(own_home == (first + i).astype(F32), shrink, 0.0))
    spread = jnp.transpose(jnp.concatenate(spread, axis=0))
    high = spread.astype(BF16)
    low = (spread - high.astype(F32)).astype(BF16)

    def expand(factors):
        flat = factors.reshape(n * held * rank, narrow)
        return jnp.dot(high, flat, preferred_element_type=F32) + jnp.dot(
            low, flat, preferred_element_type=F32
        )

    base_copy.wait_recv()
    level_ups[0].wait_recv()
    own = expand(ups[0:2]) + base[t * 2 + y] + base_in[y]
    half[t, y] = own.astype(BF16)
    for copy in level_ups[1:]:
        copy.wait_recv()
    other = expand(ups[2:4]) + base[t * 2 + 1 - y] + base_in[1 - y]
    half[t, 1 - y] = other.astype(BF16)
    half_copy = remote(half.at[t], half.at[t], half_sem.at[0], half_sem.at[1], (y, w, 1 - t))
    half_copy.start()
    for copy in home_copies + tok_copies + up_copies + level_ups + [x_copy] + part_copies:
        copy.wait_send()
    base_copy.wait_send()
    for delta in deltas:

        @pl.when(level_exists(delta))
        def _():
            for part_of in range(2):
                down_copy(part_of, delta).wait_send()

    for distance, sign in relays:

        @pl.when(relaying(distance, sign))
        def _():
            for part_of in range(2):
                relay_copy(part_of, distance, sign).wait_send()

    half_copy.wait()
    for c in range(4):
        out_ref[:, c * narrow : (c + 1) * narrow] = half[c // 2, c % 2]


def by_gather(n, tokens, key_base_weight, down_factors, up_factors, segment_lengths, entry_adapters, adapter_store_row):
    rows, width = tokens.shape
    held, rank, _ = down_factors.shape
    outputs = key_base_weight.shape[1]
    quarter, narrow = width // 4, outputs // 4
    levels = n // 2
    anywhere = pl.BlockSpec(memory_space=pl.ANY)
    scalars = pl.BlockSpec(memory_space=pltpu.SMEM)
    dma = pltpu.SemaphoreType.DMA
    return pl.pallas_call(
        functools.partial(kernel, n),
        out_shape=jax.ShapeDtypeStruct((rows, outputs), BF16),
        in_specs=[anywhere] * 4 + [scalars] * 3,
        out_specs=pl.BlockSpec(memory_space=pltpu.VMEM),
        scratch_shapes=[
            pltpu.VMEM((rows, width), BF16),
            pltpu.VMEM((width, outputs), BF16),
            pltpu.VMEM((4, rows, narrow), F32),
            pltpu.VMEM((2, rows, narrow), F32),
            pltpu.VMEM((4 * rows, quarter), BF16),
            pltpu.VMEM((4, 8, rows), F32),
            pltpu.VMEM((levels, 2, held, rank, quarter), BF16),
            pltpu.VMEM((4, levels, held, rank, narrow), BF16),
            pltpu.VMEM((rank, 4 * rows), F32),
            pltpu.VMEM((4, rank, rows), F32),
            pltpu.VMEM((8, rank, rows), F32),
            pltpu.VMEM((2, 2, rows, narrow), BF16),
            dma((4,)),
            dma((W_PIECES,)),
            dma((4,)),
            dma((4,)),
            dma((4,)),
            dma((4,)),
            dma((levels,)),
            dma((levels,)),
            dma((5, 2)),
            dma((levels, 2)),
            dma,
            dma((levels, 2, 2)),
            dma((4,)),
            dma((4,)),
            dma((2,)),
            dma((8,)),
            dma((8,)),
            dma((2,)),
        ],
        compiler_params=pltpu.CompilerParams(
            collective_id=0, has_side_effects=True, vmem_limit_bytes=60 << 20
        ),
    )(tokens, key_base_weight, down_factors, up_factors, segment_lengths, entry_adapters, adapter_store_row)


def by_sum(tokens, key_base_weight, down_factors, up_factors, segment_lengths, entry_adapters, adapter_store_row):
    held, rank, width = down_factors.shape
    outputs = up_factors.shape[2]
    entries = entry_adapters.shape[0]
    rows = tokens.shape[0]
    positions = adapter_store_row[entry_adapters]
    mine = (positions // held == lax.axis_index("wide"))[:, None, None]
    places = positions % held
    down = jnp.where(mine, down_factors[places], jnp.zeros((), BF16))
    up = jnp.where(mine, up_factors[places], jnp.zeros((), BF16))
    down, up = lax.psum((down, up), "wide")
    ends = jnp.cumsum(segment_lengths[0])
    index = jnp.arange(rows, dtype=jnp.int32)
    entry = jnp.sum((ends[None, :] <= index[:, None]).astype(jnp.int32), axis=1)
    column = jnp.arange(entries * rank, dtype=jnp.int32) // rank
    mask = (column[None, :] == entry[:, None]).astype(F32)
    shrink = mask * lax.dot_general(
        tokens,
        down.reshape(entries * rank, width),
        (((1,), (1,)), ((), ())),
        preferred_element_type=F32,
    )
    base = jnp.dot(tokens, key_base_weight, preferred_element_type=F32)
    base, shrink = lax.psum((base, shrink), "tensor")
    flat = up.reshape(entries * rank, outputs).astype(F32)
    return (base + jnp.dot(shrink, flat, precision=lax.Precision.HIGHEST)).astype(BF16)


def solution(mesh):
    n = mesh.shape["wide"]

    def per_device(tokens, key_base_weight, down_factors, *rest):
        gathered = n * down_factors.size * 2 // 4
        paired = mesh.shape["groups"] == 2 and mesh.shape["tensor"] == 2 and n % 2 == 0
        if paired and gathered <= GATHER_LIMIT:
            return by_gather(n, tokens, key_base_weight, down_factors, *rest)
        return by_sum(tokens, key_base_weight, down_factors, *rest)

    in_specs = (
        P(("groups", "wide"), "tensor"),
        P("tensor", None),
        P("wide", None, "tensor"),
        P("wide", None, None),
        P(("groups", "wide"), None),
        P("groups"),
        P(),
    )
    out_specs = P(("groups", "wide"), None)
    return jax.shard_map(
        per_device, mesh=mesh, in_specs=in_specs, out_specs=out_specs, check_vma=False
    )
```

```python
import functools

import jax
import jax.numpy as jnp
from jax import lax
from jax.experimental import pallas as pl
from jax.experimental.pallas import tpu as pltpu
from jax.sharding import PartitionSpec as P

MESH = pl.DeviceIdType.MESH
F32 = jnp.float32
BF16 = jnp.bfloat16
GATHER_LIMIT = 8 << 20
W_PIECES = 4


def kernel(
    n,
    tok_hbm,
    w_hbm,
    down_hbm,
    up_hbm,
    seg_ref,
    names_ref,
    rows_ref,
    out_ref,
    tok,
    weight,
    base,
    base_in,
    level_tok,
    level_home,
    chunks,
    ups,
    total,
    part,
    part_in,
    half,
    local_sem,
    w_sem,
    home_send,
    home_recv,
    tok_send,
    tok_recv,
    up_send,
    up_recv,
    down_send,
    down_recv,
    x_sem,
    relay_send,
    upl_send,
    upl_recv,
    base_sem,
    part_send,
    part_recv,
    half_sem,
):
    y = lax.axis_index("groups")
    w = lax.axis_index("wide")
    t = lax.axis_index("tensor")
    x = lax.rem(w, 2)
    z = w // 2
    levels = n // 2
    rows, width = tok_hbm.shape
    held, rank, _ = down_hbm.shape
    outputs = w_hbm.shape[1]
    quarter = width // 4
    narrow = outputs // 4
    entries = names_ref.shape[0]

    def level_peer(m):
        px = 1 - x if m & 1 else x
        py = 1 - y if m & 2 else y
        return py, w - x + px, px

    def quarter_of(py, px):
        return pl.ds(pl.multiple_of((py * 2 + px) * quarter, quarter), quarter)

    def columns(core, yy):
        return pl.ds(pl.multiple_of((core * 2 + yy) * narrow, narrow), narrow)

    mine = quarter_of(y, x)
    local = [
        pltpu.make_async_copy(tok_hbm, tok, local_sem.at[0]),
        pltpu.make_async_copy(tok_hbm.at[:, mine], level_tok.at[pl.ds(0, rows)], local_sem.at[1]),
        pltpu.make_async_copy(down_hbm.at[:, :, mine], chunks.at[z, 0], local_sem.at[2]),
        pltpu.make_async_copy(up_hbm.at[:, :, columns(t, y)], ups.at[0, 0], local_sem.at[3]),
    ]
    piece = width // W_PIECES
    w_copies = [
        pltpu.make_async_copy(
            w_hbm.at[pl.ds(i * piece, piece)], weight.at[pl.ds(i * piece, piece)], w_sem.at[i]
        )
        for i in range(W_PIECES)
    ]

    barrier = pltpu.get_barrier_semaphore()
    peers = [(y, lax.rem(z + k, levels) * 2 + x, t) for k in range(1, levels)]
    peers += [(level_peer(m)[0], level_peer(m)[1], t) for m in range(1, 4)]
    peers += [(level_peer(m)[0], level_peer(m)[1], 1 - t) for m in range(4)]
    for peer in peers:
        pl.semaphore_signal(barrier, inc=1, device_id=peer, device_id_type=MESH)
    for copy in local + w_copies:
        copy.start()

    lane = lax.broadcasted_iota(jnp.int32, (8, rows), 1)
    end = seg_ref[0, 0]
    home = jnp.full((8, rows), rows_ref[names_ref[0]].astype(F32), F32)
    for e in range(1, entries):
        home = jnp.where(lane >= end, rows_ref[names_ref[e]].astype(F32), home)
        end = end + seg_ref[0, e]
    level_home[0] = home

    pl.semaphore_wait(barrier, len(peers))

    def remote(src, dst, send, recv, peer):
        return pltpu.make_async_remote_copy(
            src_ref=src, dst_ref=dst, send_sem=send, recv_sem=recv, device_id=peer, device_id_type=MESH
        )

    home_copies, tok_copies = [], []
    for m in range(1, 4):
        py, pw, px = level_peer(m)
        home_copies.append(
            remote(level_home.at[0], level_home.at[m], home_send.at[m], home_recv.at[m], (py, pw, t))
        )
        tok_copies.append(
            remote(
                tok_hbm.at[:, quarter_of(py, px)],
                level_tok.at[pl.ds(m * rows, rows)],
                tok_send.at[m],
                tok_recv.at[m],
                (py, pw, t),
            )
        )
    up_copies = []
    for k in range(1, levels):
        up_copies.append(
            remote(
                up_hbm.at[:, :, columns(t, y)],
                ups.at[0, k],
                up_send.at[k],
                up_recv.at[k],
                (y, lax.rem(z + k, levels) * 2 + x, t),
            )
        )
    x_copy = remote(
        down_hbm.at[:, :, quarter_of(y, 1 - x)],
        chunks.at[z, 1],
        x_sem,
        down_recv.at[z, 1],
        (y, w - x + 1 - x, t),
    )

    def down_copy(part_of, delta):
        source = chunks.at[z, 1] if part_of else down_hbm.at[:, :, mine]
        return remote(
            source,
            chunks.at[z, part_of],
            down_send.at[delta + 2, part_of],
            down_recv.at[z, part_of],
            (y, w + 2 * delta, t),
        )

    def relay_copy(part_of, distance, sign):
        source = z + sign * distance
        return remote(
            chunks.at[source, part_of],
            chunks.at[source, part_of],
            relay_send.at[distance, (sign + 1) // 2, part_of],
            down_recv.at[source, part_of],
            (y, w - 2 * sign, t),
        )

    def arrival(level, part_of):
        return pltpu.make_async_copy(
            chunks.at[level, part_of], chunks.at[level, part_of], down_recv.at[level, part_of]
        )

    deltas = [d for d in (2, -2, 1, -1) if abs(d) < levels]
    relays = [(d, sign) for d in range(2, levels - 1) for sign in (1, -1)]

    def level_exists(delta):
        return jnp.logical_and(z + delta >= 0, z + delta < levels)

    def relaying(distance, sign):
        return jnp.logical_and(level_exists(sign * distance), level_exists(-sign))

    for copy in home_copies:
        copy.start()
    x_copy.start()
    for copy in up_copies:
        copy.start()
    for delta in deltas:

        @pl.when(level_exists(delta))
        def _():
            down_copy(0, delta).start()

    for copy in tok_copies:
        copy.start()
    local[0].wait()
    for i in range(W_PIECES):
        w_copies[i].wait()
        term = jnp.dot(
            tok[:, i * piece : (i + 1) * piece],
            weight[i * piece : (i + 1) * piece, :],
            preferred_element_type=F32,
        )
        for c in range(4):
            cut = term[:, c * narrow : (c + 1) * narrow]
            base[c] = cut if i == 0 else base[c] + cut
    base_copy = remote(
        base.at[pl.ds((1 - t) * 2, 2)], base_in, base_sem.at[0], base_sem.at[1], (y, w, 1 - t)
    )
    base_copy.start()
    x_copy.wait_recv()
    for delta in deltas:

        @pl.when(level_exists(delta))
        def _():
            down_copy(1, delta).start()

    for distance, sign in relays:

        @pl.when(relaying(distance, sign))
        def _():
            for part_of in range(2):
                copy = relay_copy(part_of, distance, sign)
                arrival(z + sign * distance, part_of).wait()
                copy.start()

    for copy in up_copies:
        copy.wait_recv()
    local[3].wait()
    level_ups = []
    for m in range(1, 4):
        py, pw, _ = level_peer(m)
        level_ups.append(remote(ups.at[0], ups.at[m], upl_send.at[m], upl_recv.at[m], (py, pw, t)))
    for copy in level_ups:
        copy.start()

    for copy in home_copies:
        copy.wait_recv()
    for copy in tok_copies:
        copy.wait_recv()
    for copy in local[1:3]:
        copy.wait()
    level_rows = 4 * rows
    home_all = jnp.concatenate([level_home[m, 0:1, :] for m in range(4)], axis=1)
    home_all = jnp.broadcast_to(home_all, (rank, level_rows))
    total[...] = jnp.zeros((rank, level_rows), F32)

    def add_shrink(level):
        product = lax.dot_general(
            chunks[level].reshape(2 * held * rank, quarter),
            level_tok[...],
            (((1,), (1,)), ((), ())),
            preferred_element_type=F32,
        )
        kept = total[...]
        for part_of in range(2):
            first = (level * 2 + (1 - x if part_of else x)) * held
            for i in range(held):
                row = (first + i).astype(F32)
                at = (part_of * held + i) * rank
                kept = kept + jnp.where(home_all == row, product[at : at + rank], 0.0)
        total[...] = kept

    add_shrink(z)
    low_end = z < levels // 2
    ahead = jnp.where(low_end, z, levels - 1 - z)
    for j in range(levels - 1):
        place = j + (j >= ahead).astype(jnp.int32)
        level = jnp.where(low_end, place, levels - 1 - place)
        forwarded = jnp.bool_(False)
        for distance, sign in relays:
            here = jnp.logical_and(relaying(distance, sign), level == z + sign * distance)
            forwarded = jnp.logical_or(forwarded, here)

        @pl.when(jnp.logical_not(forwarded))
        def _():
            for part_of in range(2):
                arrival(level, part_of).wait()

        add_shrink(level)
    for m in range(4):
        part[m] = total[:, m * rows : (m + 1) * rows]
    part_copies = []
    for m in range(4):
        py, pw, _ = level_peer(m)
        for other in range(2):
            if m == 0 and other == 0:
                continue
            slot = 2 * m + other
            core = 1 - t if other else t
            part_copies.append(
                remote(part.at[m], part_in.at[slot], part_send.at[slot], part_recv.at[slot], (py, pw, core))
            )
    for copy in part_copies:
        copy.start()

    shrink = part[0]
    for slot, copy in enumerate(part_copies, 1):
        copy.wait_recv()
        shrink = shrink + part_in[slot]
    own_home = jnp.broadcast_to(level_home[0, 0:1, :], (rank, rows))
    spread = []
    for px in (x, 1 - x):
        for k in range(levels):
            first = (lax.rem(z + levels - k, levels) * 2 + px) * held
            for i in range(held):
                spread.append(jnp.where(own_home == (first + i).astype(F32), shrink, 0.0))
    spread = jnp.transpose(jnp.concatenate(spread, axis=0))
    high = spread.astype(BF16)
    low = (spread - high.astype(F32)).astype(BF16)

    def expand(factors):
        flat = factors.reshape(n * held * rank, narrow)
        return jnp.dot(high, flat, preferred_element_type=F32) + jnp.dot(
            low, flat, preferred_element_type=F32
        )

    base_copy.wait_recv()
    level_ups[0].wait_recv()
    own = expand(ups[0:2]) + base[t * 2 + y] + base_in[y]
    half[t, y] = own.astype(BF16)
    for copy in level_ups[1:]:
        copy.wait_recv()
    other = expand(ups[2:4]) + base[t * 2 + 1 - y] + base_in[1 - y]
    half[t, 1 - y] = other.astype(BF16)
    half_copy = remote(half.at[t], half.at[t], half_sem.at[0], half_sem.at[1], (y, w, 1 - t))
    half_copy.start()
    for copy in home_copies + tok_copies + up_copies + level_ups + [x_copy] + part_copies:
        copy.wait_send()
    base_copy.wait_send()
    for delta in deltas:

        @pl.when(level_exists(delta))
        def _():
            for part_of in range(2):
                down_copy(part_of, delta).wait_send()

    for distance, sign in relays:

        @pl.when(relaying(distance, sign))
        def _():
            for part_of in range(2):
                relay_copy(part_of, distance, sign).wait_send()

    half_copy.wait()
    for c in range(4):
        out_ref[:, c * narrow : (c + 1) * narrow] = half[c // 2, c % 2]


def by_gather(n, tokens, key_base_weight, down_factors, up_factors, segment_lengths, entry_adapters, adapter_store_row):
    rows, width = tokens.shape
    held, rank, _ = down_factors.shape
    outputs = key_base_weight.shape[1]
    quarter, narrow = width // 4, outputs // 4
    levels = n // 2
    anywhere = pl.BlockSpec(memory_space=pl.ANY)
    scalars = pl.BlockSpec(memory_space=pltpu.SMEM)
    dma = pltpu.SemaphoreType.DMA
    return pl.pallas_call(
        functools.partial(kernel, n),
        out_shape=jax.ShapeDtypeStruct((rows, outputs), BF16),
        in_specs=[anywhere] * 4 + [scalars] * 3,
        out_specs=pl.BlockSpec(memory_space=pltpu.VMEM),
        scratch_shapes=[
            pltpu.VMEM((rows, width), BF16),
            pltpu.VMEM((width, outputs), BF16),
            pltpu.VMEM((4, rows, narrow), F32),
            pltpu.VMEM((2, rows, narrow), F32),
            pltpu.VMEM((4 * rows, quarter), BF16),
            pltpu.VMEM((4, 8, rows), F32),
            pltpu.VMEM((levels, 2, held, rank, quarter), BF16),
            pltpu.VMEM((4, levels, held, rank, narrow), BF16),
            pltpu.VMEM((rank, 4 * rows), F32),
            pltpu.VMEM((4, rank, rows), F32),
            pltpu.VMEM((8, rank, rows), F32),
            pltpu.VMEM((2, 2, rows, narrow), BF16),
            dma((4,)),
            dma((W_PIECES,)),
            dma((4,)),
            dma((4,)),
            dma((4,)),
            dma((4,)),
            dma((levels,)),
            dma((levels,)),
            dma((5, 2)),
            dma((levels, 2)),
            dma,
            dma((levels, 2, 2)),
            dma((4,)),
            dma((4,)),
            dma((2,)),
            dma((8,)),
            dma((8,)),
            dma((2,)),
        ],
        compiler_params=pltpu.CompilerParams(
            collective_id=0, has_side_effects=True, vmem_limit_bytes=60 << 20
        ),
    )(tokens, key_base_weight, down_factors, up_factors, segment_lengths, entry_adapters, adapter_store_row)


def by_sum(tokens, key_base_weight, down_factors, up_factors, segment_lengths, entry_adapters, adapter_store_row):
    held, rank, width = down_factors.shape
    outputs = up_factors.shape[2]
    entries = entry_adapters.shape[0]
    rows = tokens.shape[0]
    positions = adapter_store_row[entry_adapters]
    mine = (positions // held == lax.axis_index("wide"))[:, None, None]
    places = positions % held
    down = jnp.where(mine, down_factors[places], jnp.zeros((), BF16))
    up = jnp.where(mine, up_factors[places], jnp.zeros((), BF16))
    down, up = lax.psum((down, up), "wide")
    ends = jnp.cumsum(segment_lengths[0])
    index = jnp.arange(rows, dtype=jnp.int32)
    entry = jnp.sum((ends[None, :] <= index[:, None]).astype(jnp.int32), axis=1)
    column = jnp.arange(entries * rank, dtype=jnp.int32) // rank
    mask = (column[None, :] == entry[:, None]).astype(F32)
    shrink = mask * lax.dot_general(
        tokens,
        down.reshape(entries * rank, width),
        (((1,), (1,)), ((), ())),
        preferred_element_type=F32,
    )
    base = jnp.dot(tokens, key_base_weight, preferred_element_type=F32)
    base, shrink = lax.psum((base, shrink), "tensor")
    flat = up.reshape(entries * rank, outputs).astype(F32)
    return (base + jnp.dot(shrink, flat, precision=lax.Precision.HIGHEST)).astype(BF16)


def solution(mesh):
    n = mesh.shape["wide"]

    def per_device(tokens, key_base_weight, down_factors, *rest):
        gathered = n * down_factors.size * 2 // 4
        paired = mesh.shape["groups"] == 2 and mesh.shape["tensor"] == 2 and n % 2 == 0
        if paired and gathered <= GATHER_LIMIT:
            return by_gather(n, tokens, key_base_weight, down_factors, *rest)
        return by_sum(tokens, key_base_weight, down_factors, *rest)

    in_specs = (
        P(("groups", "wide"), "tensor"),
        P("tensor", None),
        P("wide", None, "tensor"),
        P("wide", None, None),
        P(("groups", "wide"), None),
        P("groups"),
        P(),
    )
    out_specs = P(("groups", "wide"), None)
    return jax.shard_map(
        per_device, mesh=mesh, in_specs=in_specs, out_specs=out_specs, check_vma=False
    )
```
